32 devices in a mesh: row: 4 (over y, core), col: 8 (over z, x).
Axes of the slice: x: 2, y: 2, z: 4, core: 2. Of those that a mesh axis runs over, the one named last changes fastest.
Arguments:
- child_fronts: float32 [2, 8192, 8192], P(None, 'row', 'col'), as said below
- parent_front: float32 [12288, 12288], P('row', 'col'), as said below
- child_map: int32 [2, 7168], replicated, may hold values from 0 to 12287, as said below
Outputs:
- child_factor: float32 [2, 8192, 1024], P(None, 'row', 'col')
- parent_factor: float32 [12288, 256], P('row', 'col')
- parent_schur: float32 [12288, 12288], P('row', 'col')
The draws below stay inside these ranges and needn't reach their ends.
Inputs may be any that keep to these rules, and one draw needn't show every extreme that they name: child_fronts[k] and parent_front are symmetric positive definite. parent_front is symmetric positive definite. The entries of child_map[k] are distinct. Each aligned block of 1024 entries of child_map[k] names exactly 128 indices in each aligned block of 1536 parent indices.
All inputs are finite; a program needn't handle non-finite values.
Results may differ from the reference program's by a relative error of at most 0.0003.
Values sent between devices are 32-bit elements; how exact they have to be, the bound alone decides.
A program may use at most 256 MiB of HBM per device.

```python
import jax
import jax.numpy as jnp
from jax import lax

WC = 8192
WP = 12288
PC = 1024
PP = 256
NB = 256
NS = 7168
CCOLS = 1024
PCOLS = 1536
QCOL = 128
N_COL = 8


def spd_matrix(key, width):
    base_key = jax.random.fold_in(key, 0)
    shift_key = jax.random.fold_in(key, 1)
    vector_key = jax.random.fold_in(key, 3)
    base = jax.random.normal(base_key, (width, width), jnp.float32)
    gram = jnp.dot(base, base.T, precision=lax.Precision.HIGHEST)
    shift = jax.random.uniform(shift_key, (width,), jnp.float32, 0.25, 1.0) * width
    direction = jax.random.normal(vector_key, (width,), jnp.float32)
    coupling = 0.5 * width * (direction[:, None] * direction[None, :])
    matrix = (gram + jnp.diag(shift) + coupling) / jnp.sqrt(jnp.float32(width))
    matrix = 0.5 * (matrix + matrix.T)
    return matrix


def draw_child_fronts(key, part):
    return jnp.stack([spd_matrix(jax.random.fold_in(key, 11 + which), WC) for which in range(2)], axis=0)


def draw_parent_front(key, part):
    return spd_matrix(jax.random.fold_in(key, 29), WP)


def one_map(key):
    source_blocks = NS // CCOLS
    dest_key, place_key = jax.random.split(key)
    dest_keys = jax.random.split(dest_key, N_COL)
    offsets = jax.vmap(lambda single: jax.random.permutation(single, PCOLS))(dest_keys)
    offsets = offsets[:, :source_blocks * QCOL].reshape(N_COL, source_blocks, QCOL)
    bases = (jnp.arange(N_COL, dtype=jnp.int32) * PCOLS)[:, None, None]
    values = jnp.transpose(offsets.astype(jnp.int32) + bases, (1, 0, 2)).reshape(source_blocks, CCOLS)
    place_keys = jax.random.split(place_key, source_blocks)
    places = jax.vmap(lambda single: jax.random.permutation(single, CCOLS))(place_keys)
    inverse = jnp.argsort(places, axis=1)
    mapped = jnp.take_along_axis(values, inverse, axis=1)
    return mapped.reshape(NS).astype(jnp.int32)


def draw_child_map(key, part):
    return jnp.stack([one_map(jax.random.fold_in(key, 47 + which)) for which in range(2)], axis=0)


def setup_inputs(seed: int = 0) -> dict:
    seeds = jax.random.split(jax.random.key(seed), 4)
    return {
        "child_fronts": draw_child_fronts(jax.random.fold_in(seeds[3], 71), 0),
        "parent_front": draw_parent_front(jax.random.fold_in(seeds[3], 71), 0),
        "child_map": draw_child_map(jax.random.fold_in(seeds[3], 71), 0),
    }


def eliminate_panels(front, pivots):
    width = front.shape[0]
    panels = []
    for panel_step in range(pivots // NB):
        offset = panel_step * NB
        corner = front[offset:offset + NB, offset:offset + NB]
        factor = jnp.linalg.cholesky(corner)
        below = front[offset:, offset:offset + NB]
        solved = jax.scipy.linalg.solve_triangular(factor, below.T, lower=True).T
        update = jnp.dot(solved, solved.T, precision=lax.Precision.HIGHEST)
        front = front.at[offset:, offset:].add(-update)
        panels.append(jnp.concatenate([jnp.zeros((offset, NB), jnp.float32), solved], axis=0))
    return (front, jnp.concatenate(panels, axis=1))

def reference(child_fronts, parent_front, child_map):
    merged = parent_front
    factors = []
    for which_child in range(2):
        updated, panels = eliminate_panels(child_fronts[which_child], PC)
        factors.append(panels)
        schur = updated[PC:, PC:]
        targets = child_map[which_child]
        merged = merged.at[targets[:, None], targets[None, :]].add(schur)
    child_factor = jnp.stack(factors, axis=0)
    updated, parent_factor = eliminate_panels(merged, PP)
    index = jnp.arange(WP, dtype=jnp.int32)
    keep = (index[:, None] >= PP) & (index[None, :] >= PP)
    parent_schur = jnp.where(keep, updated, jnp.float32(0.0))
    return (child_factor, parent_factor, parent_schur)
```

```python
from functools import partial

import jax
import jax.numpy as jnp
from jax import lax
from jax.experimental import pallas as pl
from jax.experimental.pallas import tpu as pltpu
from jax.sharding import PartitionSpec as P

PP = 256
SUB = 128
FULL = lax.Precision.HIGHEST
THREE = lax.Precision.HIGH
CONTRACT_LAST = (((1,), (1,)), ((), ()))


def mul_t(a, b, precision=FULL):
    return lax.dot_general(
        a, b, CONTRACT_LAST, precision=precision, preferred_element_type=jnp.float32
    )


def inverse_factors(blocks):
    lane = lax.broadcasted_iota(jnp.int32, (8, SUB), 1)
    sub = lax.broadcasted_iota(jnp.int32, (8, SUB), 0)
    groups = SUB // 8
    work = [[block[8 * g : 8 * g + 8, :] for g in range(groups)] for block in blocks]
    for k in range(SUB):
        first, r = divmod(k, 8)
        for m in work:
            row = m[first][r : r + 1, :]
            scaled = jnp.where(lane[0:1] == k, 1.0, row) / row[:, k : k + 1]
            scaled = jnp.broadcast_to(scaled, (8, SUB))
            for g in range(first, groups):
                if g == first and r == 7:
                    continue
                col = jnp.broadcast_to(m[g][:, k : k + 1], (8, SUB))
                if g == first:
                    below = sub > r
                    col = jnp.where(below, col, 0.0)
                    base = jnp.where((lane == k) & below, 0.0, m[g])
                else:
                    base = jnp.where(lane == k, 0.0, m[g])
                m[g] = base - col * scaled
    results = []
    for m in work:
        rows = []
        for g in range(groups):
            spot = sub + 8 * g
            diag = jnp.sum(jnp.where(lane == spot, m[g], 0.0), axis=1, keepdims=True)
            unit = jnp.where(lane < spot, m[g], jnp.where(lane == spot, 1.0, 0.0))
            rows.append(unit * lax.rsqrt(jnp.broadcast_to(diag, (8, SUB))))
        results.append(jnp.concatenate(rows, axis=0))
    return results


def factor_kernel(members, width, tall, chunk, a_ref, x_ref, out_ref, work_ref, panel_ref):
    steps = width // SUB
    work_ref[...] = a_ref[...]
    out_ref[...] = x_ref[...]

    def step(p, carry):
        at = pl.multiple_of(p * SUB, SUB)
        cols = pl.ds(at, SUB)
        inverses = inverse_factors([work_ref[k, cols, cols] for k in range(members)])
        for k in range(members):
            inverse = inverses[k]
            solved = mul_t(work_ref[k, :, cols], inverse)
            rows = lax.broadcasted_iota(jnp.int32, (width, SUB), 0)
            panel_ref[k] = jnp.where(rows >= at + SUB, solved, 0.0)

            def trailing(b, c):
                spot = pl.ds(pl.multiple_of(b * SUB, SUB), SUB)
                work_ref[k, spot, :] -= mul_t(panel_ref[k, spot, :], panel_ref[k])
                return c

            lax.fori_loop(p + 1, steps, trailing, 0)

            def own(b, c):
                spot = pl.ds(pl.multiple_of(b * chunk, chunk), chunk)
                ours = mul_t(out_ref[k, spot, cols], inverse)
                out_ref[k, spot, :] -= mul_t(ours, panel_ref[k])
                out_ref[k, spot, cols] = ours
                return c

            lax.fori_loop(0, tall // chunk, own, 0)
        return carry

    lax.fori_loop(0, steps, step, 0)


def factor_rows(corner, rows):
    members, width, _ = corner.shape
    tall = rows.shape[1]
    chunk = min(tall, 256)
    vmem = pl.BlockSpec(memory_space=pltpu.VMEM)
    return pl.pallas_call(
        partial(factor_kernel, members, width, tall, chunk),
        out_shape=jax.ShapeDtypeStruct(rows.shape, jnp.float32),
        in_specs=[vmem, vmem],
        out_specs=vmem,
        scratch_shapes=[
            pltpu.VMEM((members, width, width), jnp.float32),
            pltpu.VMEM((members, width, SUB), jnp.float32),
        ],
        compiler_params=pltpu.CompilerParams(vmem_limit_bytes=48 * 1024 * 1024),
    )(corner, rows)


def take_rows(block, picks):
    return jax.vmap(lambda one, at: jnp.take(one, at, axis=0, mode="clip"))(block, picks)


def local(child_fronts, parent_front, child_map):
    nr = lax.axis_size("row")
    nc = lax.axis_size("col")
    i = lax.axis_index("row")
    j = lax.axis_index("col")
    members, tr, tc = child_fronts.shape
    prow, pcol = parent_front.shape
    width = tr * nr
    pivots = width - child_map.shape[1]
    pb = pivots // tc
    nb = nc
    q = tc // nc
    js = nc // nr
    br = tr // tc

    with jax.named_scope("orders"):
        positions = jnp.arange(width, dtype=jnp.int32)
        full_map = jnp.concatenate(
            [jnp.zeros((members, pivots), jnp.int32), child_map], axis=1
        )
        keys = jnp.where(positions[None] < pivots, (positions % tc)[None] // q, full_map // pcol)
        order = jnp.argsort(keys.reshape(members, nb, tc), axis=2, stable=True)
        targets = jnp.take_along_axis(full_map.reshape(members, nb, tc), order, axis=2)
        targets = targets.reshape(members, nb, nc, q)

        def slots(tgt):
            flat = tgt[pb:].reshape(-1)
            fill = jnp.full((pcol,), nb * q, jnp.int32)
            return fill.at[flat].set(jnp.arange(flat.shape[0], dtype=jnp.int32) + pb * q)

        def slots_of(block):
            rel = jnp.take(targets, block, axis=2) - block * pcol
            return jax.vmap(slots)(rel)

        row_slots = [slots_of(i * js + s) for s in range(js)]
        col_slots = slots_of(j)

    with jax.named_scope("corner"):
        pieces = []
        for b in range(pb):
            mine = jnp.where((i == 0) & (j == b), child_fronts[:, :pivots, :], 0.0)
            pieces.append(lax.psum(mine, ("row", "col")))
        corner = jnp.concatenate(pieces, axis=2)

    with jax.named_scope("own_rows"):
        own_order = jnp.take(order, j, axis=1)
        strips = take_rows(jnp.swapaxes(child_fronts[:, :pivots, :], 1, 2), own_order)
        strips = strips.reshape(members, nr, tc // nr, pivots)
        own = jnp.where(i == 0, strips[:, 0], 0.0)
        for t in range(1, nr):
            own = own + lax.ppermute(strips[:, t], "row", [(0, t)])

    with jax.named_scope("exchange"):
        row_order = lax.dynamic_slice_in_dim(order, i * br, br, axis=1)
        row_order = row_order + (jnp.arange(br, dtype=jnp.int32) * tc)[None, :, None]
        row_order = row_order.reshape(members, br, nr, js * q)
        row_order = jnp.swapaxes(row_order, 1, 2).reshape(members, tr)
        picked = take_rows(child_fronts, row_order)
        picked = take_rows(jnp.swapaxes(picked, 1, 2), own_order)
        outgoing = picked.reshape(members, nc, q, nr, br * js * q)
        outgoing = jnp.transpose(outgoing, (3, 1, 0, 2, 4)).reshape(
            nr * nc, members, q, br * js * q
        )
        arrived = lax.all_to_all(outgoing, ("row", "col"), split_axis=0, concat_axis=0, tiled=True)
        arrived = arrived.reshape(nr, nc, members, q, br, js, q)
        arrived = jnp.transpose(arrived, (2, 1, 3, 5, 0, 4, 6)).reshape(
            members, nc * q, js * nb * q
        )

    with jax.named_scope("child_factor"):
        factor = factor_rows(corner, own)
        place = jnp.take(order, j, axis=1).reshape(members, nr, tc // nr)
        place = jnp.take(place, i, axis=1) + j * tc
        panel_start = (jnp.arange(pivots, dtype=jnp.int32) // 256) * 256
        factor = jnp.where(place[:, :, None] >= panel_start[None, None, :], factor, 0.0)

    with jax.named_scope("factor_rows"):
        gathered = lax.all_gather(factor, "col", axis=0, tiled=False)
        gathered = gathered.reshape(nc, members, js, q, pivots)
        owner = j // js
        cross = jnp.take(gathered, j % js, axis=2)
        cross = lax.psum(jnp.where(i == owner, cross, 0.0), "row")

        def placed(rows, slots):
            flat = jnp.swapaxes(rows, 0, 1).reshape(members, nb * q, pivots)
            got = take_rows(flat, slots)
            got = jnp.where((slots < nb * q)[:, :, None], got, 0.0)
            return jnp.concatenate([got[k] for k in range(members)], axis=1)

        left = jnp.concatenate(
            [placed(gathered[:, :, s], row_slots[s]) for s in range(js)], axis=0
        )
        right = placed(cross, col_slots)

    with jax.named_scope("place"):
        row_all = jnp.concatenate(
            [
                jnp.where(row_slots[s] < nb * q, row_slots[s] + s * nb * q, js * nb * q)
                for s in range(js)
            ],
            axis=1,
        )
        by_col = take_rows(arrived, col_slots)
        by_col = jnp.where((col_slots < nb * q)[:, :, None], by_col, 0.0)
        by_row = take_rows(jnp.swapaxes(by_col, 1, 2), row_all)
        by_row = jnp.where((row_all < js * nb * q)[:, :, None], by_row, 0.0)
        base = parent_front
        for k in range(members):
            base = base + by_row[k]

    with jax.named_scope("parent_strips"):
        row_strip = base[:PP, :] - mul_t(left[:PP], right, THREE)
        col_strip = base[:, :PP] - mul_t(left, right[:PP], THREE)
        row_strip = lax.psum(jnp.where(i == 0, row_strip, 0.0), "row")
        col_strip = lax.psum(jnp.where(j == 0, col_strip, 0.0), "col")
        head = lax.psum(jnp.where((i == 0) & (j == 0), col_strip[:PP], 0.0), ("row", "col"))

    with jax.named_scope("merged"):
        merged = base - mul_t(left, right, THREE)

    with jax.named_scope("parent_factor"):
        rows = jnp.concatenate([col_strip, row_strip.T], axis=0)
        solved = factor_rows(head[None], rows[None])[0]
        solved_rows = solved[:prow]
        solved_cols = solved[prow:]

    with jax.named_scope("parent_schur"):
        global_rows = i * prow + jnp.arange(prow, dtype=jnp.int32)
        global_cols = j * pcol + jnp.arange(pcol, dtype=jnp.int32)
        keep = (global_rows[:, None] >= PP) & (global_cols[None, :] >= PP)
        schur = jnp.where(keep, merged - mul_t(solved_rows, solved_cols, THREE), 0.0)

    with jax.named_scope("outputs"):
        share = PP // nc
        parent_factor = lax.dynamic_slice_in_dim(solved_rows, j * share, share, axis=1)
        cshare = pivots // nc
        pieces = factor.reshape(members, tc // nr, nc, cshare)
        pieces = lax.all_to_all(pieces, "col", split_axis=2, concat_axis=0, tiled=False)
        pieces = pieces.reshape(nr, br, members, tc // nr, cshare)
        pieces = lax.all_to_all(pieces, "row", split_axis=0, concat_axis=0, tiled=True)
        pieces = jnp.transpose(pieces, (2, 1, 0, 3, 4)).reshape(members, tr, cshare)
        natural = jnp.argsort(lax.dynamic_slice_in_dim(order, i * br, br, axis=1), axis=2)
        natural = natural + (jnp.arange(br, dtype=jnp.int32) * tc)[None, :, None]
        child_factor = take_rows(pieces, natural.reshape(members, tr))
    return (child_factor, parent_factor, schur)


def solution(mesh):
    return jax.shard_map(
        local,
        mesh=mesh,
        in_specs=(P(None, "row", "col"), P("row", "col"), P()),
        out_specs=(P(None, "row", "col"), P("row", "col"), P("row", "col")),
        check_vma=False,
    )
```
